32 devices in a mesh: dp: 8 (over z, y), blk: 4 (over x, core).
Axes of the slice: x: 2, y: 2, z: 4, core: 2. Of those that a mesh axis runs over, the one named last changes fastest.
Arguments:
- token_ids: int32 [8, 128], P('dp'), may hold values from 0 to 50303
- lengths: int32 [8, 16], P('dp'), may hold values from 0 to 128, as said below
- embedding: float32 [50304, 768], P(('dp', 'blk'))
- emb_mean: float32 [50304, 768], P(('dp', 'blk')), may hold values from -9.536743e-07 to 9.536743e-07
- emb_var: float32 [50304, 768], P(('dp', 'blk')), may hold values from 1.1348653e-13 to 1.8332438e-12
- positions: float32 [128, 768], replicated, may hold values from -0.12 to 0.12
- pos_mean: float32 [128, 768], replicated, may hold values from -1.9073486e-06 to 1.9073486e-06
- pos_var: float32 [128, 768], replicated, may hold values from 2.2959198e-13 to 3.6664877e-12
- gains_biases: float32 [14, 768], replicated
- gains_mean: float32 [14, 768], replicated, may hold values from -7.6293945e-06 to 7.6293945e-06
- gains_var: float32 [14, 768], replicated, may hold values from 3.6664877e-12 to 5.8489213e-11
- w_attn: float32 [1, 768, 4, 768], P(None, 'blk', None, 'dp')
- attn_mean: float32 [1, 768, 4, 768], P(None, 'blk', None, 'dp'), may hold values from -1.9073486e-06 to 1.9073486e-06
- attn_var: float32 [1, 768, 4, 768], P(None, 'blk', None, 'dp'), may hold values from 2.2959198e-13 to 3.6664877e-12
- w_fc: float32 [1, 768, 3072], P(None, 'blk', 'dp'), may hold values from -0.21875 to 0.21875
- fc_mean: float32 [1, 768, 3072], P(None, 'blk', 'dp'), may hold values from -1.9073486e-06 to 1.9073486e-06
- fc_var: float32 [1, 768, 3072], P(None, 'blk', 'dp'), may hold values from 2.2959198e-13 to 3.6664877e-12
- w_proj: float32 [1, 3072, 768], P(None, 'blk', 'dp'), may hold values from -0.109375 to 0.109375
- proj_mean: float32 [1, 3072, 768], P(None, 'blk', 'dp'), may hold values from -1.9073486e-06 to 1.9073486e-06
- proj_var: float32 [1, 3072, 768], P(None, 'blk', 'dp'), may hold values from 2.2959198e-13 to 3.6664877e-12
Outputs:
- loss_sum: float32 [], replicated
- token_count: float32 [], replicated
- grad_norm: float32 [], replicated
- emb_grad: float32 [50304, 768], P(('dp', 'blk'))
- emb_var_new: float32 [50304, 768], P(('dp', 'blk'))
- emb_new: float32 [50304, 768], P(('dp', 'blk'))
- pos_grad: float32 [128, 768], replicated
- pos_var_new: float32 [128, 768], replicated
- pos_new: float32 [128, 768], replicated
- gains_grad: float32 [14, 768], replicated
- gains_var_new: float32 [14, 768], replicated
- gains_new: float32 [14, 768], replicated
- attn_grad: float32 [1, 768, 4, 768], P(None, 'blk', None, 'dp')
- attn_var_new: float32 [1, 768, 4, 768], P(None, 'blk', None, 'dp')
- attn_new: float32 [1, 768, 4, 768], P(None, 'blk', None, 'dp')
- fc_grad: float32 [1, 768, 3072], P(None, 'blk', 'dp')
- fc_var_new: float32 [1, 768, 3072], P(None, 'blk', 'dp')
- fc_new: float32 [1, 768, 3072], P(None, 'blk', 'dp')
- proj_grad: float32 [1, 3072, 768], P(None, 'blk', 'dp')
- proj_var_new: float32 [1, 3072, 768], P(None, 'blk', 'dp')
- proj_new: float32 [1, 3072, 768], P(None, 'blk', 'dp')
The draws below stay inside these ranges and needn't reach their ends.
Inputs may be any that keep to these rules, and one draw needn't show every extreme that they name: Each row holds its packed documents' lengths in order; their sum is the row's live length and the rest of the row is padding. In one row a single document fills all 128 positions.
All inputs are finite; a program needn't handle non-finite values. Where the reference program divides by a largest or mean magnitude, that divisor is 1e-20 or more.
Results may differ from the reference program's by a relative error of at most 0.0095.
The reference program's roundings to bfloat16 on the way count: a program that leaves them out, or rounds other values in their place, can miss the bound.
Values may be sent and summed in bfloat16 or wider, within the bound.
No kernel may reach another device: no remote copies, remote signals or barrier semaphores. Data moves between devices by JAX's collectives and lax.ppermute only.
A program may use at most 384 MiB of HBM per device.

```python
import math
import jax
import jax.numpy as jnp
import numpy as np
from jax import lax

D = 768
HEADS = 12
HDIM = 64
FF = 3072
VOCAB = 50304
TOK_DEV = 128
DOCS = 16
LAYERS = 1
NS_ITERS = 2
STEP = 10
ROWS = 8
VDP = 6288
SMALL_ROWS = 14
NPARAM = 45820416


def draw_lengths(key, part):
    key = jax.random.fold_in(key, 11)
    live_key, exponent_key, extra_key, chosen_key = jax.random.split(key, 4)
    row_index = jnp.arange(ROWS, dtype=jnp.int32)
    live_len = TOK_DEV // 3 + 2 * TOK_DEV // 3 * row_index // max(ROWS - 1, 1) - jax.random.randint(live_key, (ROWS,), 0, TOK_DEV // 8 + 1)
    top_exponent = max(int(math.log2(TOK_DEV)) - 1, 1)
    exponent = jax.random.randint(exponent_key, (ROWS, DOCS), 0, top_exponent)
    base_len = jnp.left_shift(jnp.ones_like(exponent), exponent)
    raw_len = base_len + jax.random.randint(extra_key, (ROWS, DOCS), 0, base_len)
    before = jnp.cumsum(raw_len, 1, dtype=jnp.int32) - raw_len
    taken_len = jnp.clip(live_len[:, None] - before, 0, raw_len)
    rest_len = live_len - jnp.sum(taken_len[:, :-1], 1, dtype=jnp.int32)
    packed = jnp.concatenate([taken_len[:, :-1], rest_len[:, None]], 1).astype(jnp.int32)
    chosen_row = jax.random.randint(chosen_key, (), 0, ROWS)
    full_row = jnp.where(jnp.arange(DOCS, dtype=jnp.int32) == 0, TOK_DEV, 0).astype(jnp.int32)
    return jnp.where((row_index == chosen_row)[:, None], full_row[None, :], packed).astype(jnp.int32)


def draw_embedding(key, part):
    key = jax.random.fold_in(key, 5)
    within = (jnp.arange(VOCAB) % VDP).astype(jnp.float32) / VDP
    base_val = jax.random.normal(key, (VOCAB, D), jnp.float32)
    row_scale = 1.0 + 2.0 * within
    return (base_val * row_scale[:, None] / math.sqrt(D)).astype(jnp.float32)


def draw_gains_biases(key, part):
    key = jax.random.fold_in(key, 7)
    gain_key, bias_key = jax.random.split(key)
    per_layer = 8 + FF // D
    row_index = jnp.arange(SMALL_ROWS)
    row_kind = row_index % per_layer
    gain_row = (row_index < LAYERS * per_layer) & ((row_kind == 0) | (row_kind == 5)) | (row_index == LAYERS * per_layer)
    ramp_val = 0.5 + jnp.arange(D).astype(jnp.float32) / D
    noise_val = jax.random.normal(gain_key, (SMALL_ROWS, D), jnp.float32)
    bias_val = 0.2 * jax.random.normal(bias_key, (SMALL_ROWS, D), jnp.float32)
    return jnp.where(gain_row[:, None], ramp_val[None, :] * (1.0 + 0.1 * noise_val), bias_val).astype(jnp.float32)


def draw_w_attn(key, part):
    key = jax.random.fold_in(key, 9)
    slot_scale = jnp.array([1.0, 1.0, 1.0, 4.0], jnp.float32)
    base_val = jax.random.normal(key, (LAYERS, D, 4, D), jnp.float32)
    return (base_val * slot_scale[None, None, :, None] / math.sqrt(D)).astype(jnp.float32)


def touch_ends(result, stream_key, least, largest):
    shape = result.shape
    spot = [jax.random.randint(jax.random.fold_in(stream_key, axis), (), 0, shape[axis]) for axis in range(len(shape))]
    result = result.at[tuple(spot)].set(least)
    longest = shape.index(max(shape))
    spot[longest] = (spot[longest] + 1) % shape[longest]
    return result.at[tuple(spot)].set(largest)


def level_of(rng, extent, cuts, low, largest):
    level = 1.0
    for dim, blocks in cuts:
        heights = jax.random.uniform(jax.random.fold_in(jax.random.fold_in(rng, 6), dim), (blocks,), jnp.float32, low / len(cuts), largest / len(cuts))
        level = level * jnp.repeat(jnp.exp(heights), extent[dim] // blocks).reshape((-1,) + (1,) * (len(extent) - 1 - dim))
    return level


def rank_bounds(number_of, lean):
    portions = [(1 << 20) // math.isqrt(grade ** lean) + 1 for grade in range(1, number_of + 1)]
    scale = 1 + sum(portions) // (1 << 30)
    return np.cumsum(np.array([max(1, weight // scale) for weight in portions]))


def skewed_ids(rng, extent, count, lean):
    table = rank_bounds(count, lean)
    pick = jax.random.randint(jax.random.fold_in(rng, 1), extent, 0, int(table[count - 1]))
    standing = jnp.searchsorted(jnp.asarray(table, jnp.int32), pick, side="right")
    return jax.random.permutation(jax.random.fold_in(rng, 2), count)[standing].astype(jnp.int32)


def bell_draw(stream_key, shape, width, bound, cuts=(), kind=jnp.bfloat16):
    loudness = level_of(stream_key, shape, cuts, -0.22, 0.18) if cuts else 1.0
    result = jax.random.normal(stream_key, shape, jnp.float32) * width * loudness
    return jnp.minimum(jnp.maximum(result, -bound), bound).astype(kind)


def setup_inputs(seed: int = 0) -> dict:
    keys = jax.random.split(jax.random.key(seed), 21)
    token_ids = touch_ends(skewed_ids(keys[0], (ROWS, TOK_DEV), VOCAB, 2), jax.random.fold_in(keys[0], 3), 0, VOCAB - 1).astype(jnp.int32)
    lengths = draw_lengths(jax.random.fold_in(keys[20], 71), 0)
    embedding = draw_embedding(jax.random.fold_in(keys[20], 71), 0)
    emb_mean = bell_draw(keys[3], (VOCAB, D), (0.055 * 0.02 / NPARAM ** 0.5), 9.5367431640625e-07, ((0, 32),), jnp.float32)
    emb_var = jnp.clip(jnp.exp(math.log(1.8332438431883924e-12) - 2.7821581 * jax.random.uniform(keys[4], (VOCAB, D), jnp.float32) ** level_of(keys[4], (VOCAB, D), ((0, 32),), -0.2, 0.2)), 1.1348653137024933e-13, 1.8332438431883924e-12)
    positions = bell_draw(keys[5], (TOK_DEV, D), 0.02, 0.12, (), jnp.float32)
    pos_mean = bell_draw(keys[6], (TOK_DEV, D), (0.111 * 0.02 / NPARAM ** 0.5), 1.9073486328125e-06, (), jnp.float32)
    pos_var = jnp.clip(jnp.exp(jax.random.uniform(keys[7], (TOK_DEV, D), jnp.float32, math.log(2.295919801931917e-13), math.log(3.666487686376785e-12))), 2.295919801931917e-13, 3.666487686376785e-12)
    gains_biases = draw_gains_biases(jax.random.fold_in(keys[20], 71), 0)
    gains_mean = bell_draw(keys[9], (SMALL_ROWS, D), (0.444 * 0.02 / NPARAM ** 0.5), 7.62939453125e-06, (), jnp.float32)
    gains_var = jnp.clip(jnp.exp(jax.random.uniform(keys[10], (SMALL_ROWS, D), jnp.float32, math.log(3.666487686376785e-12), math.log(5.848921347251235e-11))), 3.666487686376785e-12, 5.848921347251235e-11)
    w_attn = draw_w_attn(jax.random.fold_in(keys[20], 71), 0)
    attn_mean = bell_draw(keys[12], (LAYERS, D, 4, D), (0.111 * 0.02 / NPARAM ** 0.5), 1.9073486328125e-06, ((1, 4), (3, 8)), jnp.float32)
    attn_var = jnp.clip(jnp.exp(math.log(3.666487686376785e-12) - 2.7706857 * jax.random.uniform(keys[13], (LAYERS, D, 4, D), jnp.float32) ** level_of(keys[13], (LAYERS, D, 4, D), ((1, 4), (3, 8)), -0.2, 0.2)), 2.295919801931917e-13, 3.666487686376785e-12)
    w_fc = bell_draw(keys[14], (LAYERS, D, FF), D ** -0.5, 0.21875, ((1, 4), (2, 8)), jnp.float32)
    fc_mean = bell_draw(keys[15], (LAYERS, D, FF), (0.111 * 0.02 / NPARAM ** 0.5), 1.9073486328125e-06, ((1, 4), (2, 8)), jnp.float32)
    fc_var = jnp.clip(jnp.exp(math.log(3.666487686376785e-12) - 2.7706857 * jax.random.uniform(keys[16], (LAYERS, D, FF), jnp.float32) ** level_of(keys[16], (LAYERS, D, FF), ((1, 4), (2, 8)), -0.2, 0.2)), 2.295919801931917e-13, 3.666487686376785e-12)
    w_proj = bell_draw(keys[17], (LAYERS, FF, D), FF ** -0.5, 0.109375, ((1, 4), (2, 8)), jnp.float32)
    proj_mean = bell_draw(keys[18], (LAYERS, FF, D), (0.111 * 0.02 / NPARAM ** 0.5), 1.9073486328125e-06, ((1, 4), (2, 8)), jnp.float32)
    proj_var = jnp.clip(jnp.exp(math.log(3.666487686376785e-12) - 2.7706857 * jax.random.uniform(keys[19], (LAYERS, FF, D), jnp.float32) ** level_of(keys[19], (LAYERS, FF, D), ((1, 4), (2, 8)), -0.2, 0.2)), 2.295919801931917e-13, 3.666487686376785e-12)
    return dict(token_ids=token_ids, lengths=lengths, embedding=embedding, emb_mean=emb_mean, emb_var=emb_var, positions=positions, pos_mean=pos_mean, pos_var=pos_var, gains_biases=gains_biases, gains_mean=gains_mean, gains_var=gains_var, w_attn=w_attn, attn_mean=attn_mean, attn_var=attn_var, w_fc=w_fc, fc_mean=fc_mean, fc_var=fc_var, w_proj=w_proj, proj_mean=proj_mean, proj_var=proj_var)


@jax.custom_vjp
def low(v):
    return lax.optimization_barrier(v.astype(jnp.bfloat16)).astype(jnp.float32)

@jax.custom_vjp
def low_back(v):
    return v

def low_keep(v):
    return (low(v), None)

def low_pass(kept, grad):
    return (grad,)

def back_keep(v):
    return (v, None)

def back_low(kept, grad):
    return (low(grad),)
low.defvjp(low_keep, low_pass)
low_back.defvjp(back_keep, back_low)
HIGHEST = lax.Precision.HIGHEST
ln_eps = 1e-05
zloss_weight = 0.01
damping = 0.1
clip_level = 0.02
learn_rate = 0.1
beta_first = 0.9
beta_second = 0.95
adam_eps = 1e-08
weight_decay = 0.1

def layer_norm(values, gain_vec, shift_vec):
    centered = values - lax.optimization_barrier(jnp.mean(values, -1, keepdims=True))
    spread = lax.optimization_barrier(jnp.mean(centered * centered, -1, keepdims=True))
    return centered * lax.rsqrt(spread + ln_eps) * gain_vec + shift_vec

def both_round(values):
    return low(low_back(values))

def doc_layout(lengths_row, row_len):
    doc_ends = jnp.cumsum(lengths_row, dtype=jnp.int32)
    spot_index = jnp.arange(row_len, dtype=jnp.int32)
    after_end = doc_ends[None, :] <= spot_index[:, None]
    segment = lax.optimization_barrier(jnp.sum(after_end.astype(jnp.int32), 1, dtype=jnp.int32))
    start_pos = lax.optimization_barrier(jnp.sum(jnp.where(after_end, lengths_row[None, :], 0), 1, dtype=jnp.int32))
    local_pos = (spot_index - start_pos).astype(jnp.int32)
    live_len = doc_ends[-1]
    next_seg = jnp.concatenate([segment[1:], jnp.full((1,), -1, jnp.int32)])
    counted = (spot_index + 1 < live_len) & (next_seg == segment)
    attn_mask = (spot_index[None, :] <= spot_index[:, None]) & (segment[None, :] == segment[:, None])
    return (local_pos, counted, attn_mask)

def small_rows(gains_biases, layer_index):
    per_layer = 8 + FF // D
    base_row = layer_index * per_layer
    fc_bias = gains_biases[base_row + 7:base_row + 7 + FF // D].reshape(FF)
    return (gains_biases[base_row], gains_biases[base_row + 1], gains_biases[base_row + 2], gains_biases[base_row + 3], gains_biases[base_row + 4], gains_biases[base_row + 5], gains_biases[base_row + 6], fc_bias, gains_biases[base_row + 7 + FF // D])

def adam_update(weights, mean_old, var_old, gradient, clip_factor, decay):
    clipped = clip_factor * gradient
    new_mean = beta_first * mean_old + (1.0 - beta_first) * clipped
    new_var = beta_second * var_old + (1.0 - beta_second) * clipped * clipped
    mean_hat = new_mean / (1.0 - beta_first ** STEP)
    var_hat = new_var / (1.0 - beta_second ** STEP)
    updated = weights - learn_rate * (mean_hat / (jnp.sqrt(var_hat) + adam_eps) + decay * weights)
    return (clipped, new_var, updated)

def attend_rows(queries, key_rows, value_rows, attn_mask):
    score_scale = 1.0 / math.sqrt(HDIM)
    scores = low_back(jnp.einsum('rshd,rthd->rhst', queries, key_rows, precision=HIGHEST) * score_scale)
    scores = jnp.where(attn_mask[:, None], scores, -1e+30)
    attn_probs = low(jax.nn.softmax(scores, axis=-1))
    return both_round(jnp.einsum('rhst,rthd->rshd', attn_probs, value_rows, precision=HIGHEST))

def forward_loss(embedding, positions, gains_biases, w_attn, w_fc, w_proj, taps, token_ids, local_pos, counted, targets, attn_mask, total_count):
    row_total, seq_len = token_ids.shape
    table_low = low(embedding)
    stream = low_back(table_low[token_ids]) + positions[local_pos]
    kept_all = []
    for layer_index in range(LAYERS):
        gain_one, shift_one, bias_q, bias_v, bias_o, gain_two, shift_two, bias_fc, bias_proj = small_rows(gains_biases, layer_index)
        attn_low = low(w_attn[layer_index])
        fc_low = low(w_fc[layer_index])
        proj_low = low(w_proj[layer_index])
        normed = low(layer_norm(stream, gain_one, shift_one))
        qkv_bias = jnp.stack([bias_q, jnp.zeros_like(bias_q), bias_v])
        qkv_low = both_round(jnp.einsum('rsd,dke->rske', normed, attn_low[:, :3], precision=HIGHEST) + qkv_bias + taps[0][layer_index])
        head_split = qkv_low.reshape(row_total, seq_len, 3, HEADS, HDIM)
        mixed_out = attend_rows(head_split[:, :, 0], head_split[:, :, 1], head_split[:, :, 2], attn_mask).reshape(row_total, seq_len, D)
        stream = stream + low_back(jnp.einsum('rsd,de->rse', mixed_out, attn_low[:, 3], precision=HIGHEST) + bias_o + taps[1][layer_index])
        normed_two = low(layer_norm(stream, gain_two, shift_two))
        hidden = low_back(jnp.einsum('rsd,df->rsf', normed_two, fc_low, precision=HIGHEST) + bias_fc + taps[2][layer_index])
        active = low(jax.nn.gelu(hidden, approximate=True))
        stream = stream + low_back(jnp.einsum('rsf,fd->rsd', active, proj_low, precision=HIGHEST) + bias_proj + taps[3][layer_index])
        kept_all.append((normed, mixed_out, normed_two, active))
    final_row = LAYERS * (8 + FF // D)
    final_low = low(layer_norm(stream, gains_biases[final_row], gains_biases[final_row + 1]))

    def head_block(block_args):
        final_block, target_block, counted_block = block_args
        logits = low_back(jnp.dot(final_block, table_low.T, precision=HIGHEST))
        log_total = jax.nn.logsumexp(logits, axis=-1)
        target_logit = jnp.take_along_axis(logits, target_block[:, None], axis=1)[:, 0]
        terms = log_total - target_logit + zloss_weight * log_total * log_total
        return jnp.sum(jnp.where(counted_block, terms, 0.0))
    loss_sum = jnp.sum(lax.map(jax.checkpoint(head_block), (final_low, targets, counted)))
    return (loss_sum / total_count, (loss_sum, kept_all))

def gram_matrix(values):
    flat_rows = values.reshape(-1, values.shape[-1])
    return jnp.dot(flat_rows.T, flat_rows, precision=HIGHEST)

def approx_inverse(factor):
    order = factor.shape[-1]
    identity = jnp.eye(order, dtype=jnp.float32)
    row_scale = lax.optimization_barrier(jnp.max(lax.optimization_barrier(jnp.sum(jnp.abs(factor), -1)), -1)) + 1e-06
    shifted = factor / row_scale[..., None, None] + damping * identity
    kappa_val = 1.0 + damping
    inverse = 2.0 / kappa_val * identity - shifted / (kappa_val * kappa_val)
    shifted_low = low(shifted)
    for sweep_index in range(NS_ITERS - 1):
        inverse_low = low(inverse)
        product = low(jnp.matmul(shifted_low, inverse_low, precision=HIGHEST))
        inverse = 2.0 * inverse - jnp.matmul(product, inverse_low, precision=HIGHEST)
    return inverse

def precondition(left_inv, gradient, right_inv):
    return jnp.dot(left_inv, jnp.dot(gradient, right_inv, precision=HIGHEST), precision=HIGHEST)

def reference(token_ids, lengths, embedding, emb_mean, emb_var, positions, pos_mean, pos_var, gains_biases, gains_mean, gains_var, w_attn, attn_mean, attn_var, w_fc, fc_mean, fc_var, w_proj, proj_mean, proj_var):
    row_total, seq_len = token_ids.shape
    local_pos, counted, attn_mask = jax.vmap(lambda lengths_row: doc_layout(lengths_row, seq_len))(lengths)
    targets = jnp.concatenate([token_ids[:, 1:], jnp.zeros((row_total, 1), jnp.int32)], 1)
    total_count = jnp.sum(counted.astype(jnp.float32))
    tokens = float(row_total * seq_len)
    taps = (jnp.zeros((LAYERS, row_total, seq_len, 3, D), jnp.float32), jnp.zeros((LAYERS, row_total, seq_len, D), jnp.float32), jnp.zeros((LAYERS, row_total, seq_len, FF), jnp.float32), jnp.zeros((LAYERS, row_total, seq_len, D), jnp.float32))

    def loss_of(*params):
        return forward_loss(*params, token_ids, local_pos, counted, targets, attn_mask, total_count)
    loss_value, pullback, (loss_sum, kept_all) = jax.vjp(loss_of, embedding, positions, gains_biases, w_attn, w_fc, w_proj, taps, has_aux=True)
    d_table, d_pos, d_small, d_attn, d_fc, d_proj, d_taps = pullback(jnp.ones_like(loss_value))
    grad_scale = total_count * total_count / tokens
    a_small, g_small, a_large, g_large = ([], [], [], [])
    for layer_index in range(LAYERS):
        normed, mixed_out, normed_two, active = kept_all[layer_index]
        a_small.append(jnp.stack([gram_matrix(normed), gram_matrix(mixed_out), gram_matrix(normed_two)]) / tokens)
        qkv_grad = d_taps[0][layer_index]
        g_small.append(jnp.stack([gram_matrix(qkv_grad[:, :, 0]), gram_matrix(qkv_grad[:, :, 1]), gram_matrix(qkv_grad[:, :, 2]), gram_matrix(d_taps[1][layer_index]), gram_matrix(d_taps[3][layer_index])]) * grad_scale)
        a_large.append(gram_matrix(active) / tokens)
        g_large.append(gram_matrix(d_taps[2][layer_index]) * grad_scale)
    inv_small = approx_inverse(jnp.concatenate([jnp.stack(a_small), jnp.stack(g_small)], 1))
    inv_large = approx_inverse(jnp.stack([jnp.stack(a_large), jnp.stack(g_large)], 1))
    pre_attn = jnp.stack([jnp.stack([precondition(inv_small[layer_index, 0 if part_index < 3 else 1], d_attn[layer_index, :, part_index], inv_small[layer_index, 3 + part_index]) for part_index in range(4)], 1) for layer_index in range(LAYERS)])
    pre_fc = jnp.stack([precondition(inv_small[layer_index, 2], d_fc[layer_index], inv_large[layer_index, 1]) for layer_index in range(LAYERS)])
    pre_proj = jnp.stack([precondition(inv_large[layer_index, 0], d_proj[layer_index], inv_small[layer_index, 7]) for layer_index in range(LAYERS)])
    squares = jnp.sum(pre_attn * pre_attn) + jnp.sum(pre_fc * pre_fc) + jnp.sum(pre_proj * pre_proj) + jnp.sum(d_table * d_table) + jnp.sum(d_pos * d_pos) + jnp.sum(d_small * d_small)
    grad_norm = jnp.sqrt(squares)
    clip_factor = clip_level / jnp.maximum(grad_norm, clip_level)
    emb_out = adam_update(embedding, emb_mean, emb_var, d_table, clip_factor, weight_decay)
    pos_out = adam_update(positions, pos_mean, pos_var, d_pos, clip_factor, weight_decay)
    gains_out = adam_update(gains_biases, gains_mean, gains_var, d_small, clip_factor, 0.0)
    attn_out = adam_update(w_attn, attn_mean, attn_var, pre_attn, clip_factor, weight_decay)
    fc_out = adam_update(w_fc, fc_mean, fc_var, pre_fc, clip_factor, weight_decay)
    proj_out = adam_update(w_proj, proj_mean, proj_var, pre_proj, clip_factor, weight_decay)
    return (loss_sum, total_count, grad_norm, emb_out[0], emb_out[1], emb_out[2], pos_out[0], pos_out[1], pos_out[2], gains_out[0], gains_out[1], gains_out[2], attn_out[0], attn_out[1], attn_out[2], fc_out[0], fc_out[1], fc_out[2], proj_out[0], proj_out[1], proj_out[2])
```

```python
import math

import jax
import jax.numpy as jnp
from jax import lax
from jax.sharding import PartitionSpec as P

D = 768
HEADS = 12
HDIM = 64
FF = 3072
STEP = 10

HIGHEST = lax.Precision.HIGHEST
ln_eps = 1e-05
zloss_weight = 0.01
damping = 0.1
clip_level = 0.02
learn_rate = 0.1
beta_first = 0.9
beta_second = 0.95
adam_eps = 1e-08
weight_decay = 0.1
kappa = 1.0 + damping
bf16 = jnp.bfloat16
f32 = jnp.float32


def dot(spec, left, right):
    return jnp.einsum(spec, left, right, preferred_element_type=f32)


def xor_permute(value, axis, bit):
    size = lax.axis_size(axis)
    return lax.ppermute(value, axis, [(k, k ^ bit) for k in range(size)])


def spread(value, axes):
    count = 1
    for name in axes if isinstance(axes, tuple) else (axes,):
        count *= lax.axis_size(name)
    copies = jnp.broadcast_to(value[None], (count,) + value.shape)
    return lax.all_to_all(copies, axes, split_axis=0, concat_axis=0)


def by_order(bit, mine, other, axis):
    first = jnp.where(bit == 0, mine, other)
    second = jnp.where(bit == 0, other, mine)
    return jnp.stack([first, second], axis)


def layer_norm(values, gain_vec, shift_vec):
    centered = values - jnp.mean(values, -1, keepdims=True)
    spread_val = jnp.mean(centered * centered, -1, keepdims=True)
    return centered * lax.rsqrt(spread_val + ln_eps) * gain_vec + shift_vec


def norm_back(values, gain_vec, cotangent):
    centered = values - jnp.mean(values, -1, keepdims=True)
    rstd = lax.rsqrt(jnp.mean(centered * centered, -1, keepdims=True) + ln_eps)
    unit = centered * rstd
    scaled = cotangent * gain_vec
    result = rstd * (
        scaled
        - jnp.mean(scaled, -1, keepdims=True)
        - unit * jnp.mean(scaled * unit, -1, keepdims=True)
    )
    return result, jnp.sum(cotangent * unit, 0), jnp.sum(cotangent, 0)


def doc_layout(lengths_row, row_len):
    doc_ends = jnp.cumsum(lengths_row, dtype=jnp.int32)
    spot_index = jnp.arange(row_len, dtype=jnp.int32)
    after_end = doc_ends[None, :] <= spot_index[:, None]
    segment = jnp.sum(after_end.astype(jnp.int32), 1, dtype=jnp.int32)
    start_pos = jnp.sum(jnp.where(after_end, lengths_row[None, :], 0), 1, dtype=jnp.int32)
    local_pos = spot_index - start_pos
    live_len = doc_ends[-1]
    next_seg = jnp.concatenate([segment[1:], jnp.full((1,), -1, jnp.int32)])
    counted = (spot_index + 1 < live_len) & (next_seg == segment)
    attn_mask = (spot_index[None, :] <= spot_index[:, None]) & (
        segment[None, :] == segment[:, None]
    )
    return (local_pos, counted, attn_mask)


def adam_update(weights, mean_old, var_old, gradient, clip_factor, decay):
    clipped = clip_factor * gradient
    new_mean = beta_first * mean_old + (1.0 - beta_first) * clipped
    new_var = beta_second * var_old + (1.0 - beta_second) * clipped * clipped
    mean_hat = new_mean / (1.0 - beta_first**STEP)
    var_hat = new_var / (1.0 - beta_second**STEP)
    updated = weights - learn_rate * (mean_hat / (jnp.sqrt(var_hat) + adam_eps) + decay * weights)
    return (clipped, new_var, updated)


def approx_inverse(tokens_low, scale):
    factor = dot("td,te->de", tokens_low, tokens_low) * scale
    order = factor.shape[0]
    top = jnp.max(jnp.sum(jnp.abs(factor), -1)) + 1e-06
    eye = jnp.eye(order, dtype=f32)
    shifted = factor / top + damping * eye
    start = 2.0 / kappa * eye - shifted / (kappa * kappa)
    start_low = start.astype(bf16)
    product = dot("ij,jk->ik", shifted.astype(bf16), start_low).astype(bf16)
    return 2.0 * start - dot("ij,jk->ik", product, start_low)


def series():
    alpha = 2.0 / kappa - damping / (kappa * kappa)
    beta = 1.0 / (kappa * kappa)
    return (
        2.0 * alpha - damping * alpha * alpha,
        -2.0 * beta - alpha * alpha + 2.0 * alpha * beta * damping,
        2.0 * alpha * beta - damping * beta * beta,
        -beta * beta,
    )


def sum_half(partial, core_bit):
    rows = partial.shape[0]
    halves = partial.reshape(2, rows // 2, partial.shape[1])
    keep = lax.dynamic_index_in_dim(halves, core_bit, 0, False)
    send = lax.dynamic_index_in_dim(halves, 1 - core_bit, 0, False)
    keep = keep + xor_permute(send, "blk", 1)
    return keep + xor_permute(keep, "blk", 2)


def join_half(half, core_bit):
    other = xor_permute(half, "blk", 1)
    both = by_order(core_bit, half, other, 0)
    return both.reshape((2 * half.shape[0],) + half.shape[1:])


def split_dots(left_low, right):
    high = right.astype(bf16)
    rest = (right - high.astype(f32)).astype(bf16)
    return jnp.dot(left_low, high, preferred_element_type=f32) + jnp.dot(
        left_low, rest, preferred_element_type=f32
    )


def body(
    token_ids,
    lengths,
    embedding,
    emb_mean,
    emb_var,
    positions,
    pos_mean,
    pos_var,
    gains_biases,
    gains_mean,
    gains_var,
    w_attn,
    attn_mean,
    attn_var,
    w_fc,
    fc_mean,
    fc_var,
    w_proj,
    proj_mean,
    proj_var,
):
    row_len = token_ids.shape[1]
    piece_rows = embedding.shape[0]
    dp_size = lax.axis_size("dp")
    blk_size = lax.axis_size("blk")
    dp_index = lax.axis_index("dp")
    blk_index = lax.axis_index("blk")
    core_bit = blk_index % 2
    chip_bit = blk_index // 2
    tokens = float(row_len * dp_size)
    sub_len = row_len // blk_size
    half_len = row_len // 2
    total_rows = row_len * dp_size
    ff_part = FF // blk_size
    head_cols = D // blk_size
    col_part = D // dp_size
    wide_part = FF // dp_size

    packed = spread(jnp.concatenate([token_ids[0], lengths[0]]), "dp")
    every_ids = packed[:, :row_len]
    every_lengths = packed[:, row_len:]
    every_local, every_counted, _ = jax.vmap(lambda row: doc_layout(row, row_len))(every_lengths)
    total_count = jnp.sum(every_counted.astype(f32))
    _, _, attn_mask = doc_layout(lengths[0], row_len)
    every_targets = jnp.concatenate([every_ids[:, 1:], jnp.zeros((dp_size, 1), jnp.int32)], 1)
    row_base = (dp_index * blk_size + blk_index) * piece_rows
    vocab_slots = row_base + jnp.arange(piece_rows, dtype=jnp.int32)
    table_low = embedding.astype(bf16)

    attn_low = w_attn[0].astype(bf16)
    qkv_all = lax.all_gather(attn_low[:, :3], "dp", axis=0)
    out_all = lax.all_gather(attn_low[:, 3], "dp", axis=0)
    fc_all = lax.all_gather(w_fc[0].astype(bf16), "dp", axis=0)
    proj_all = lax.all_gather(w_proj[0].astype(bf16), "dp", axis=0)
    span = dp_size // blk_size

    def turn(value):
        grouped = value.reshape((blk_size, span) + value.shape[1:])
        return lax.all_to_all(grouped, "blk", split_axis=0, concat_axis=0)

    qkv_turn = turn(qkv_all)
    w_qkv = jnp.transpose(qkv_turn, (0, 2, 3, 1, 4)).reshape(D, 3, head_cols)
    fc_turn = turn(fc_all)
    w_up = jnp.transpose(fc_turn, (0, 2, 1, 3)).reshape(D, ff_part)
    w_out = jnp.transpose(out_all, (1, 0, 2)).reshape(head_cols, D)
    w_down = jnp.transpose(proj_all, (1, 0, 2)).reshape(ff_part, D)

    def sub_of(index):
        return (index % 2) * (blk_size // 2) + index // 2

    id_subs = every_ids.reshape(dp_size, blk_size, sub_len)

    def picked(step):
        ids = lax.dynamic_index_in_dim(id_subs, sub_of(blk_index ^ step), 1, False).reshape(-1)
        hit = (ids[:, None] == vocab_slots[None, :]).astype(bf16)
        return jnp.dot(hit, table_low, preferred_element_type=f32).astype(bf16)

    far = jnp.stack([picked(1), picked(3)])
    near = jnp.stack([picked(0), picked(2)])
    near = near + xor_permute(far, "blk", 1)
    embedded_sub = near[0] + xor_permute(near[1], "blk", 2)
    embedded_sub = lax.all_to_all(
        embedded_sub.reshape(dp_size, sub_len, D), "dp", split_axis=0, concat_axis=0
    )
    embedded_sub = jnp.sum(embedded_sub.astype(f32), 0).astype(bf16)
    embedded = by_order(chip_bit, embedded_sub, xor_permute(embedded_sub, "blk", 2), 0)
    embedded = embedded.reshape(half_len, D).astype(f32)
    my_local, my_counted, _ = doc_layout(lengths[0], row_len)
    half_start = core_bit * half_len
    local_half = lax.dynamic_slice_in_dim(my_local, half_start, half_len, 0)
    pos_hit = (local_half[:, None] == jnp.arange(row_len, dtype=jnp.int32)[None, :]).astype(f32)
    stream = embedded + jnp.dot(pos_hit, positions, precision=HIGHEST)

    gain_one, shift_one, bias_q, bias_v, bias_o, gain_two, shift_two = (
        gains_biases[k] for k in range(7)
    )
    ff_rows = FF // D
    bias_fc = gains_biases[7 : 7 + ff_rows].reshape(FF)
    bias_proj = gains_biases[7 + ff_rows]
    gain_fin = gains_biases[8 + ff_rows]
    shift_fin = gains_biases[9 + ff_rows]

    def cut(vector, width):
        return lax.dynamic_slice_in_dim(vector, blk_index * width, width, 0)

    normed = join_half(layer_norm(stream, gain_one, shift_one).astype(bf16), core_bit)
    bias_q_cut, bias_v_cut = cut(bias_q, head_cols), cut(bias_v, head_cols)
    qkv_bias = jnp.stack([bias_q_cut, jnp.zeros_like(bias_q_cut), bias_v_cut])
    qkv_low = (dot("sd,dke->ske", normed, w_qkv) + qkv_bias).astype(bf16)
    heads_here = head_cols // HDIM
    split = qkv_low.reshape(row_len, 3, heads_here, HDIM)
    score_scale = 1.0 / math.sqrt(HDIM)
    scores = dot("shd,thd->hst", split[:, 0], split[:, 1]) * score_scale
    probs = jax.nn.softmax(jnp.where(attn_mask[None], scores, -1e30), axis=-1)
    probs_low = probs.astype(bf16)
    mixed = dot("hst,thd->shd", probs_low, split[:, 2]).astype(bf16).reshape(row_len, head_cols)
    middle = stream + sum_half(jnp.dot(mixed, w_out, preferred_element_type=f32), core_bit) + bias_o

    normed_two_half = layer_norm(middle, gain_two, shift_two).astype(bf16)
    normed_two = join_half(normed_two_half, core_bit)
    hidden = jnp.dot(normed_two, w_up, preferred_element_type=f32) + cut(bias_fc, ff_part)
    active = jax.nn.gelu(hidden, approximate=True).astype(bf16)
    stream_out = (
        middle
        + sum_half(jnp.dot(active, w_down, preferred_element_type=f32), core_bit)
        + bias_proj
    )
    final_half = layer_norm(stream_out, gain_fin, shift_fin).astype(bf16)

    final_here = spread(final_half, "dp")
    final_pair = by_order(core_bit, final_here, xor_permute(final_here, "blk", 1), 1)
    final_all = final_pair.reshape(total_rows, D)
    logits = dot("sd,vd->sv", final_all, table_low)
    target_hit = every_targets.reshape(-1)[:, None] == vocab_slots[None, :]
    top_here = jnp.max(logits, 1)
    sum_here = jnp.sum(jnp.exp(logits - top_here[:, None]), 1)
    hit_here = jnp.sum(jnp.where(target_hit, logits, 0.0), 1)
    stats = spread(jnp.stack([top_here, sum_here, hit_here]), ("dp", "blk"))
    top_all = jnp.max(stats[:, 0], 0)
    sum_all = jnp.sum(stats[:, 1] * jnp.exp(stats[:, 0] - top_all[None]), 0)
    target_logit = jnp.sum(stats[:, 2], 0)
    log_total = top_all + jnp.log(sum_all)
    flat_counted = every_counted.reshape(-1)
    loss_sum = jnp.sum(
        jnp.where(
            flat_counted, log_total - target_logit + zloss_weight * log_total * log_total, 0.0
        )
    )
    row_weight = jnp.where(flat_counted, 1.0, 0.0) / total_count
    glog = (
        row_weight[:, None]
        * (
            (1.0 + 2.0 * zloss_weight * log_total)[:, None] * jnp.exp(logits - log_total[:, None])
            - target_hit.astype(f32)
        )
    ).astype(bf16)
    head_part = jnp.dot(glog, table_low, preferred_element_type=f32)
    head_part = head_part.reshape(dp_size, 2, half_len, D)
    head_keep = lax.dynamic_index_in_dim(head_part, core_bit, 1, False)
    head_send = lax.dynamic_index_in_dim(head_part, 1 - core_bit, 1, False)
    head_keep = head_keep + xor_permute(head_send, "blk", 1)
    head_keep = head_keep.reshape(dp_size, 2, sub_len, D)
    head_send = lax.dynamic_index_in_dim(head_keep, 1 - chip_bit, 1, False).astype(bf16)
    head_keep = lax.dynamic_index_in_dim(head_keep, chip_bit, 1, False)
    head_keep = head_keep + xor_permute(head_send, "blk", 2).astype(f32)
    head_rows = lax.all_to_all(head_keep.astype(bf16), "dp", split_axis=0, concat_axis=0)
    head_sub = jnp.sum(head_rows.astype(f32), 0)
    grad_final = by_order(chip_bit, head_sub, xor_permute(head_sub, "blk", 2), 0)
    grad_final = grad_final.reshape(half_len, D)
    table_grad = dot("sv,sd->vd", glog, final_all)

    grad_out, d_gain_fin, d_shift_fin = norm_back(stream_out, gain_fin, grad_final)
    grad_proj_half = grad_out.astype(bf16)
    grad_proj = join_half(grad_proj_half, core_bit)
    grad_active = dot("sd,fd->sf", grad_proj, w_down)
    _, gelu_pull = jax.vjp(lambda value: jax.nn.gelu(value, approximate=True), hidden)
    grad_fc = gelu_pull(grad_active)[0].astype(bf16)
    back_two = sum_half(dot("sf,df->sd", grad_fc, w_up), core_bit)
    back_middle, d_gain_two, d_shift_two = norm_back(middle, gain_two, back_two)
    grad_middle = grad_out + back_middle
    grad_attn_half = grad_middle.astype(bf16)
    grad_attn = join_half(grad_attn_half, core_bit)
    grad_mixed = (
        dot("se,de->sd", grad_attn, w_out).astype(bf16).reshape(row_len, heads_here, HDIM)
    )
    grad_value = dot("hst,shd->thd", probs_low, grad_mixed)
    grad_probs = dot("shd,thd->hst", grad_mixed, split[:, 2])
    grad_scores = (
        probs * (grad_probs - jnp.sum(grad_probs * probs, -1, keepdims=True))
    ).astype(bf16)
    grad_query = dot("hst,thd->shd", grad_scores, split[:, 1]) * score_scale
    grad_key = dot("hst,shd->thd", grad_scores, split[:, 0]) * score_scale
    grad_qkv = (
        jnp.stack([grad_query, grad_key, grad_value], 1)
        .reshape(row_len, 3, head_cols)
        .astype(bf16)
    )
    back_one = sum_half(dot("ske,dke->sd", grad_qkv, w_qkv), core_bit)
    back_stream, d_gain_one, d_shift_one = norm_back(stream, gain_one, back_one)
    grad_stream = grad_middle + back_stream
    grad_embed_half = grad_stream.astype(bf16)

    pair_blocks = jnp.stack([grad_qkv[:, 0], grad_qkv[:, 1], grad_qkv[:, 2], mixed], 0)
    pair_got = lax.all_to_all(pair_blocks, "blk", split_axis=0, concat_axis=0)
    pair_got = jnp.transpose(pair_got, (1, 0, 2)).reshape(row_len, D)
    last = blk_index == blk_size - 1
    in_side = lax.all_gather(jnp.where(last, pair_got, normed), "dp", axis=0).reshape(-1, D)
    out_side = lax.all_gather(jnp.where(last, grad_attn, pair_got), "dp", axis=0).reshape(-1, D)

    def wide_half(value):
        halves = value.reshape(2, half_len, ff_part)
        keep = lax.dynamic_index_in_dim(halves, core_bit, 0, False)
        send = lax.dynamic_index_in_dim(halves, 1 - core_bit, 0, False)
        pair = by_order(core_bit, keep, xor_permute(send, "blk", 1), 1)
        pair = pair.reshape(half_len, 2 * ff_part)
        both = by_order(chip_bit, pair, xor_permute(pair, "blk", 2), 1)
        return both.reshape(half_len, FF)

    wide_rows = jnp.where(chip_bit == 0, wide_half(active), wide_half(grad_fc))
    slim_rows = jnp.where(chip_bit == 0, grad_proj_half, normed_two_half)
    wide_mine = lax.all_gather(wide_rows, "dp", axis=0).reshape(-1, FF)
    slim_mine = lax.all_gather(slim_rows, "dp", axis=0).reshape(-1, D)
    wide_pair = jnp.concatenate([wide_mine, xor_permute(wide_mine, "blk", 1)], 0)
    slim_pair = jnp.concatenate([slim_mine, xor_permute(slim_mine, "blk", 1)], 0)

    out_scale = total_count * total_count / tokens
    in_scale = 1.0 / tokens

    inv_in = approx_inverse(in_side, in_scale)
    inv_out = approx_inverse(out_side, out_scale)
    col_start = dp_index * col_part
    right = lax.dynamic_slice_in_dim(inv_out, col_start, col_part, 1)
    turned = split_dots(out_side, right)
    grad_cols = jnp.dot(
        in_side.T.astype(f32), turned, precision=HIGHEST
    )
    pre_small = jnp.dot(inv_in, grad_cols, precision=HIGHEST)

    wide_scale = jnp.where(chip_bit == 0, in_scale, out_scale)
    slim_scale = jnp.where(chip_bit == 0, out_scale, in_scale)
    inv_slim = approx_inverse(slim_pair, slim_scale)
    gram = dot("tf,sf->ts", wide_pair, wide_pair)
    trace = jnp.sum(jnp.square(wide_pair.astype(f32)))
    gram_low = (gram * (1.0 / jnp.maximum(trace, 1e-30))).astype(bf16)
    part_rows = 256
    part_first = (dp_index * 2 + core_bit) % (FF // part_rows) * part_rows
    if 2 * dp_size * part_rows < FF:
        part_rows = FF // (2 * dp_size)
        part_first = (dp_index * 2 + core_bit) * part_rows
    wide_part_cols = lax.dynamic_slice_in_dim(wide_pair, part_first, part_rows, 1)
    row_sums = jnp.sum(jnp.abs(dot("ti,tj->ij", wide_part_cols, wide_pair)), 1)
    top_part = jnp.max(row_sums) * wide_scale
    tops = spread(jnp.full((8, 128), top_part, f32), ("dp", "blk"))[:, 0, 0]
    tops = jnp.max(tops.reshape(dp_size, 2, 2), (0, 2))
    wide_top = jnp.where(chip_bit == 0, tops[0], tops[1]) + 1e-06
    slim_cols = col_part // 2
    wide_cols = wide_part // 2
    slim_right = lax.dynamic_slice_in_dim(
        inv_slim, dp_index * col_part + core_bit * slim_cols, slim_cols, 1
    )
    start_slim = split_dots(slim_pair, slim_right)
    start_slim = jnp.pad(start_slim, ((0, 0), (0, wide_cols - slim_cols)))
    start_wide = lax.dynamic_slice_in_dim(
        wide_pair, dp_index * wide_part + core_bit * wide_cols, wide_cols, 1
    ).astype(f32)
    power = jnp.where(chip_bit == 0, start_slim, start_wide)
    ratio = trace * wide_scale / wide_top
    coef = series()
    total = coef[0] * power
    factor = 1.0
    for step in range(1, 4):
        power = jnp.dot(gram_low, power.astype(bf16), preferred_element_type=f32)
        factor = factor * ratio
        total = total + (coef[step] * factor) * power
    total_slim = total[:, :slim_cols]
    pre_down = jnp.dot(wide_pair.T.astype(f32), total_slim, precision=HIGHEST)
    pre_up = jnp.dot(
        inv_slim,
        jnp.dot(slim_pair.T.astype(f32), total, precision=HIGHEST),
        precision=HIGHEST,
    )
    pre_wide = jnp.where(
        chip_bit == 0,
        pre_down.reshape(blk_size, ff_part * slim_cols),
        pre_up.reshape(blk_size, head_cols * wide_cols),
    )
    squares = jnp.sum(pre_small * pre_small) + jnp.sum(pre_wide * pre_wide)
    sent = jnp.concatenate([pre_small.reshape(blk_size, head_cols * col_part), pre_wide], 1)
    got = lax.all_to_all(sent, "blk", split_axis=0, concat_axis=0)
    small_count = head_cols * col_part
    pre_attn = jnp.transpose(
        got[:, :small_count].reshape(blk_size, head_cols, col_part), (1, 0, 2)
    )[None]
    got_wide = got[:, small_count:]
    pre_proj = jnp.concatenate(
        [got_wide[k].reshape(ff_part, slim_cols) for k in range(2)], 1
    )[None]
    pre_fc = jnp.concatenate(
        [got_wide[k].reshape(head_cols, wide_cols) for k in range(2, 4)], 1
    )[None]

    embed_here = spread(grad_embed_half, "dp")
    embed_pair = by_order(core_bit, embed_here, xor_permute(embed_here, "blk", 1), 1)
    grad_embed = embed_pair.reshape(total_rows, D)
    id_hit = (vocab_slots[:, None] == every_ids.reshape(-1)[None, :]).astype(bf16)
    table_grad = table_grad + jnp.dot(id_hit, grad_embed, preferred_element_type=f32)
    pos_all = (
        jnp.arange(row_len, dtype=jnp.int32)[:, None] == every_local.reshape(-1)[None, :]
    ).astype(bf16)
    grad_pos = jnp.dot(pos_all, grad_embed, preferred_element_type=f32)

    lead = (chip_bit == 0).astype(f32)
    token_rows = lead * jnp.stack(
        [
            d_gain_one,
            d_shift_one,
            jnp.sum(grad_attn_half.astype(f32), 0),
            d_gain_two,
            d_shift_two,
            jnp.sum(grad_proj_half.astype(f32), 0),
            d_gain_fin,
            d_shift_fin,
        ]
    )

    def place(vector, width):
        return lax.dynamic_update_slice_in_dim(
            jnp.zeros((vector.shape[0] * blk_size,), f32), vector, blk_index * width, 0
        )

    qkv_sums = jnp.sum(grad_qkv.astype(f32), 0)
    small_part = jnp.concatenate(
        [
            token_rows[:2],
            place(qkv_sums[0], head_cols)[None],
            place(qkv_sums[2], head_cols)[None],
            token_rows[2:5],
            place(jnp.sum(grad_fc.astype(f32), 0), ff_part).reshape(ff_rows, D),
            token_rows[5:],
        ],
        0,
    )
    small_part = small_part + xor_permute(small_part, "blk", 1)
    small_part = small_part + xor_permute(small_part, "blk", 2)
    grad_small = jnp.sum(spread(small_part, "dp"), 0)

    squares = squares + jnp.sum(table_grad * table_grad)
    every_squares = spread(jnp.full((8, 128), squares, f32), ("dp", "blk"))[:, 0, 0]
    all_squares = (
        jnp.sum(every_squares) + jnp.sum(grad_small * grad_small) + jnp.sum(grad_pos * grad_pos)
    )
    grad_norm = jnp.sqrt(all_squares)
    clip_factor = clip_level / jnp.maximum(grad_norm, clip_level)
    emb_out = adam_update(embedding, emb_mean, emb_var, table_grad, clip_factor, weight_decay)
    pos_out = adam_update(positions, pos_mean, pos_var, grad_pos, clip_factor, weight_decay)
    gains_out = adam_update(gains_biases, gains_mean, gains_var, grad_small, clip_factor, 0.0)
    attn_out = adam_update(w_attn, attn_mean, attn_var, pre_attn, clip_factor, weight_decay)
    fc_out = adam_update(w_fc, fc_mean, fc_var, pre_fc, clip_factor, weight_decay)
    proj_out = adam_update(w_proj, proj_mean, proj_var, pre_proj, clip_factor, weight_decay)
    return (
        (loss_sum, total_count, grad_norm)
        + emb_out
        + pos_out
        + gains_out
        + attn_out
        + fc_out
        + proj_out
    )


def solution(mesh):
    token = P("dp", None)
    table = P(("dp", "blk"), None)
    attn = P(None, "blk", None, "dp")
    flat = P(None, "blk", "dp")
    return jax.shard_map(
        body,
        mesh=mesh,
        in_specs=(token,) * 2
        + (table,) * 3
        + (P(),) * 6
        + (attn,) * 3
        + (flat,) * 6,
        out_specs=(P(),) * 3 + (table,) * 3 + (P(),) * 6 + (attn,) * 3 + (flat,) * 6,
        check_vma=False,
    )
```

```python
import functools
import math

import jax
import jax.numpy as jnp
from jax import lax
from jax.experimental import pallas as pl
from jax.experimental.pallas import tpu as pltpu
from jax.sharding import PartitionSpec as P

D = 768
HEADS = 12
HDIM = 64
FF = 3072
STEP = 10

HIGHEST = lax.Precision.HIGHEST
ln_eps = 1e-05
zloss_weight = 0.01
damping = 0.1
clip_level = 0.02
learn_rate = 0.1
beta_first = 0.9
beta_second = 0.95
adam_eps = 1e-08
weight_decay = 0.1
kappa = 1.0 + damping
bf16 = jnp.bfloat16
f32 = jnp.float32


def dot(spec, left, right):
    return jnp.einsum(spec, left, right, preferred_element_type=f32)


def xor_permute(value, axis, bit):
    size = lax.axis_size(axis)
    return lax.ppermute(value, axis, [(k, k ^ bit) for k in range(size)])


def spread(value, axes):
    count = 1
    for name in axes if isinstance(axes, tuple) else (axes,):
        count *= lax.axis_size(name)
    copies = jnp.broadcast_to(value[None], (count,) + value.shape)
    return lax.all_to_all(copies, axes, split_axis=0, concat_axis=0)


def spread_small(value, axis):
    size = lax.axis_size(axis)
    index = lax.axis_index(axis)
    found = jnp.stack([value] + [xor_permute(value, axis, k) for k in range(1, size)])
    bits = size.bit_length() - 1
    found = found.reshape((2,) * bits + value.shape)
    for place in range(bits):
        bit = index // 2 ** (bits - 1 - place) % 2
        found = jnp.where(bit == 0, found, jnp.flip(found, place))
    return found.reshape((size,) + value.shape)


def gather_half(value):
    mine = spread(value, "dp").reshape(-1, value.shape[-1])
    return mine, xor_permute(mine, "blk", 1)


def together(*values):
    return lax.optimization_barrier(values)


def by_order(bit, mine, other, axis):
    first = jnp.where(bit == 0, mine, other)
    second = jnp.where(bit == 0, other, mine)
    return jnp.stack([first, second], axis)


def layer_norm(values, gain_vec, shift_vec):
    centered = values - jnp.mean(values, -1, keepdims=True)
    spread_val = jnp.mean(centered * centered, -1, keepdims=True)
    return centered * lax.rsqrt(spread_val + ln_eps) * gain_vec + shift_vec


def norm_back(values, gain_vec, cotangent):
    centered = values - jnp.mean(values, -1, keepdims=True)
    rstd = lax.rsqrt(jnp.mean(centered * centered, -1, keepdims=True) + ln_eps)
    unit = centered * rstd
    scaled = cotangent * gain_vec
    result = rstd * (
        scaled
        - jnp.mean(scaled, -1, keepdims=True)
        - unit * jnp.mean(scaled * unit, -1, keepdims=True)
    )
    return (
        result,
        jnp.sum(cotangent * unit, 0, keepdims=True),
        jnp.sum(cotangent, 0, keepdims=True),
    )


def doc_layout(lengths_row, row_len):
    doc_ends = jnp.cumsum(lengths_row, dtype=jnp.int32)
    spot_index = jnp.arange(row_len, dtype=jnp.int32)
    after_end = doc_ends[None, :] <= spot_index[:, None]
    segment = jnp.sum(after_end.astype(jnp.int32), 1, dtype=jnp.int32)
    start_pos = jnp.sum(jnp.where(after_end, lengths_row[None, :], 0), 1, dtype=jnp.int32)
    local_pos = spot_index - start_pos
    live_len = doc_ends[-1]
    next_seg = jnp.concatenate([segment[1:], jnp.full((1,), -1, jnp.int32)])
    counted = (spot_index + 1 < live_len) & (next_seg == segment)
    attn_mask = (spot_index[None, :] <= spot_index[:, None]) & (
        segment[None, :] == segment[:, None]
    )
    return (local_pos, counted, attn_mask)


def adam_update(weights, mean_old, var_old, gradient, clip_factor, decay):
    clipped = clip_factor * gradient
    new_mean = beta_first * mean_old + (1.0 - beta_first) * clipped
    new_var = beta_second * var_old + (1.0 - beta_second) * clipped * clipped
    mean_hat = new_mean / (1.0 - beta_first**STEP)
    var_hat = new_var / (1.0 - beta_second**STEP)
    updated = weights - learn_rate * (mean_hat / (jnp.sqrt(var_hat) + adam_eps) + decay * weights)
    return (clipped, new_var, updated)


def whole():
    return pl.BlockSpec(memory_space=pltpu.VMEM)


def scalar():
    return pl.BlockSpec(memory_space=pltpu.SMEM)


SMALL = pl.CostEstimate(flops=2**20, bytes_accessed=2**16, transcendentals=0)


def params(mib):
    return pltpu.CompilerParams(vmem_limit_bytes=mib * 2**20)


def turn_dot(left, right):
    return lax.dot_general(left, right, (((0,), (0,)), ((), ())), preferred_element_type=f32)


def far_dot(left, right):
    return lax.dot_general(left, right, (((1,), (1,)), ((), ())), preferred_element_type=f32)


def gelu_value(value):
    root = math.sqrt(2.0 / math.pi)
    square = value * value
    curve = jnp.tanh(value * (root + (root * 0.044715) * square))
    return value * (0.5 + 0.5 * curve)


def gelu_slope(value):
    root = math.sqrt(2.0 / math.pi)
    square = value * value
    curve = jnp.tanh(value * (root + (root * 0.044715) * square))
    bent = value * (root + (3.0 * root * 0.044715) * square)
    return 0.5 + 0.5 * (curve + (1.0 - curve * curve) * bent)


def add_product(total_ref, piece, fresh):
    product = far_dot(piece, piece)

    @pl.when(fresh)
    def _():
        total_ref[...] = product

    @pl.when(jnp.logical_not(fresh))
    def _():
        total_ref[...] += product


def wide_sums(share, first, total_ref, wide_ref, gram_ref, top_ref):
    top = jnp.maximum(jnp.max(jnp.abs(total_ref[...])), 1e-30)
    gram_ref[...] = (total_ref[...] * (1.0 / top)).astype(bf16)
    rows = wide_ref[:, pl.ds(pl.multiple_of(first, 128), share)]

    def sums(index, carry):
        outer = pl.ds(pl.multiple_of(index * 768, 768), 768)
        return carry + jnp.sum(jnp.abs(turn_dot(rows, wide_ref[:, outer])), 1, keepdims=True)

    row_sums = lax.fori_loop(0, wide_ref.shape[1] // 768, sums, jnp.zeros((share, 1), f32))
    top_ref[0] = top
    top_ref[1] = jnp.max(row_sums)


def wide_start_kernel(parts, step, spot_ref, bias_ref, in_ref, *refs):
    up_refs = refs[:parts]
    wide_ref = refs[parts]
    half = in_ref.shape[0] // 2
    width = up_refs[0].shape[1]

    def fill(bend):
        for part in range(parts):

            def columns(index, carry, part=part):
                inner = pl.ds(pl.multiple_of(index * step, step), step)
                outer = pl.ds(pl.multiple_of(part * width + index * step, step), step)
                for base in (0, half):
                    hidden = (
                        jnp.dot(
                            in_ref[base : base + half, :],
                            up_refs[part][:, inner],
                            preferred_element_type=f32,
                        )
                        + bias_ref[pl.ds(part, 1), inner]
                    )
                    wide_ref[base : base + half, outer] = bend(hidden).astype(bf16)
                return carry

            lax.fori_loop(0, width // step, columns, 0)

    @pl.when(spot_ref[0] == 0)
    def _():
        fill(gelu_value)

    @pl.when(spot_ref[0] != 0)
    def _():
        fill(gelu_slope)


def fits(rows):
    return rows <= 1024


def plain_wide_start(spot, bias, slim_in, ups):
    pieces = []
    for part, up in enumerate(ups):
        hidden = jnp.dot(slim_in, up, preferred_element_type=f32) + bias[part]
        pieces.append(jnp.where(spot[0] == 0, gelu_value(hidden), gelu_slope(hidden)).astype(bf16))
    return jnp.concatenate(pieces, 1)


def plain_wide_back(spot, start, slim_out, downs, share):
    back = jnp.concatenate([far_dot(slim_out, down) for down in downs], 1)
    wide = jnp.where(spot[0] == 0, start, (start.astype(f32) * back).astype(bf16))
    gram = far_dot(wide, wide)
    top = jnp.maximum(jnp.max(jnp.abs(gram)), 1e-30)
    rows = lax.dynamic_slice_in_dim(wide, spot[1], share, 1)
    sums = jnp.max(jnp.sum(jnp.abs(turn_dot(rows, wide)), 1))
    return wide, (gram * (1.0 / top)).astype(bf16), jnp.stack([top, sums])


def plain_wide_finish(chip, coefs, gram, start, wide, slim_in, left, columns):
    power, total = start, coefs[0] * start
    for step in range(1, 4):
        power = jnp.dot(gram, power.astype(bf16), preferred_element_type=f32)
        total = total + coefs[step] * power
    model = slim_in.shape[1]
    high, rest = high_low(total)
    down = jnp.stack(
        [
            (turn_dot(high, piece) + turn_dot(rest, piece))[:columns]
            for piece in (wide[:, :model], wide[:, model : 2 * model])
        ]
    )
    turned = turn_dot(slim_in, high) + turn_dot(slim_in, rest)
    up = jnp.dot(left, turned, precision=HIGHEST)
    square = jnp.where(chip[0] == 0, jnp.sum(down * down), jnp.sum(up * up))
    return down, up, square.reshape(1)


def wide_start(spot, bias, slim_in, ups):
    parts = len(ups)
    rows, total = slim_in.shape[0], parts * ups[0].shape[1]
    if not fits(rows):
        return plain_wide_start(spot, bias, slim_in, ups)
    return pl.pallas_call(
        functools.partial(wide_start_kernel, parts, 256),
        out_shape=jax.ShapeDtypeStruct((rows, total), bf16),
        in_specs=[scalar()] + [whole()] * (2 + parts),
        out_specs=whole(),
        compiler_params=params(48),
        cost_estimate=SMALL,
    )(spot, bias, slim_in, *ups)


def wide_back_kernel(parts, step, share, spot_ref, start_ref, out_ref, *refs):
    down_refs = refs[:parts]
    wide_ref, gram_ref, top_ref, total_ref = refs[parts:]
    half = out_ref.shape[0] // 2
    width = down_refs[0].shape[0]

    @pl.when(spot_ref[0] == 0)
    def _():
        wide_ref[...] = start_ref[...]

        def columns(index, carry):
            outer = pl.ds(pl.multiple_of(index * width, width), width)
            add_product(total_ref, start_ref[:, outer], index == 0)
            return carry

        lax.fori_loop(0, parts, columns, 0)

    @pl.when(spot_ref[0] != 0)
    def _():
        for part in range(parts):

            def columns(index, carry, part=part):
                inner = pl.ds(pl.multiple_of(index * step, step), step)
                outer = pl.ds(pl.multiple_of(part * width + index * step, step), step)
                for base in (0, half):
                    back = far_dot(out_ref[base : base + half, :], down_refs[part][inner, :])
                    slope = start_ref[base : base + half, outer].astype(f32)
                    wide_ref[base : base + half, outer] = (slope * back).astype(bf16)
                fresh = jnp.logical_and(part == 0, index == 0)
                add_product(total_ref, wide_ref[:, outer], fresh)
                return carry

            lax.fori_loop(0, width // step, columns, 0)

    wide_sums(share, spot_ref[1], total_ref, wide_ref, gram_ref, top_ref)


def wide_back(spot, start, slim_out, downs, share):
    rows, total = start.shape
    parts = len(downs)
    if not fits(rows):
        return plain_wide_back(spot, start, slim_out, downs, share)
    return pl.pallas_call(
        functools.partial(wide_back_kernel, parts, 384, share),
        out_shape=(
            jax.ShapeDtypeStruct((rows, total), bf16),
            jax.ShapeDtypeStruct((rows, rows), bf16),
            jax.ShapeDtypeStruct((2,), f32),
        ),
        in_specs=[scalar()] + [whole()] * (2 + parts),
        out_specs=(whole(), whole(), scalar()),
        scratch_shapes=[pltpu.VMEM((rows, rows), f32)],
        compiler_params=params(56),
        cost_estimate=SMALL,
    )(spot, start, slim_out, *downs)


def lane_row(ref, first, count):
    return jnp.concatenate([ref[first + k : first + k + 1, :] for k in range(count)], 1)


def head_kernel(
    limit, step, base_ref, target_ref, counted_ref, table_ref, one, two, logit_ref, log_ref, hit_ref
):
    half = one.shape[0]
    blocks = half // 128
    starts = jnp.full((1, half), -1e30, f32)

    def places(index):
        return lax.broadcasted_iota(jnp.int32, (step, 1), 0) + index * step

    def fill(index, tops):
        rows = pl.ds(pl.multiple_of(index * step, 16), step)
        result = []
        for part, ref in enumerate((one, two)):
            value = far_dot(table_ref[rows, :], ref[...])
            value = jnp.where(places(index) < limit, value, -1e30)
            logit_ref[rows, part * half : (part + 1) * half] = value
            result.append(jnp.maximum(tops[part], jnp.max(value, 0, keepdims=True)))
        return tuple(result)

    count = table_ref.shape[0] // step
    tops = lax.fori_loop(0, count, fill, (starts, starts))
    base = base_ref[0]
    goals = [lane_row(target_ref, part * blocks, blocks) - base for part in range(2)]
    zeros = jnp.zeros((1, half), f32)

    def add_up(index, carry):
        rows = pl.ds(pl.multiple_of(index * step, 16), step)
        place = places(index)
        result = []
        for part in range(2):
            value = logit_ref[rows, part * half : (part + 1) * half]
            total, hits = carry[part]
            total += jnp.sum(jnp.exp(value - tops[part]), 0, keepdims=True)
            found = jnp.logical_and(place == goals[part], place < limit)
            hits += jnp.sum(jnp.where(found, value, 0.0), 0, keepdims=True)
            result.append((total, hits))
        return tuple(result)

    sums = lax.fori_loop(0, count, add_up, ((zeros, zeros), (zeros, zeros)))
    hit_sum = jnp.float32(0.0)
    for part in range(2):
        total, hits = sums[part]
        log_total = tops[part] + jnp.log(total)
        for k in range(blocks):
            row = part * blocks + k
            log_ref[row : row + 1, :] = log_total[:, k * 128 : (k + 1) * 128]
        hit_sum += jnp.sum(hits * lane_row(counted_ref, part * blocks, blocks))
    hit_ref[0] = hit_sum


def head_logits(base, targets, counted, table, one, two, limit):
    rows = table.shape[0]
    tokens = 2 * one.shape[0]
    return pl.pallas_call(
        functools.partial(head_kernel, limit, rows // 8),
        out_shape=(
            jax.ShapeDtypeStruct((rows, tokens), f32),
            jax.ShapeDtypeStruct((tokens // 128, 128), f32),
            jax.ShapeDtypeStruct((1,), f32),
        ),
        in_specs=[scalar()] + [whole()] * 5,
        out_specs=(whole(), whole(), scalar()),
        compiler_params=params(40),
        cost_estimate=SMALL,
    )(base, targets, counted, table, one, two)


def head_back_kernel(
    limit,
    step,
    base_ref,
    target_ref,
    weight_ref,
    log_ref,
    table_ref,
    logit_ref,
    own_ref,
    far_ref,
    glog_ref,
):
    half = own_ref.shape[0]
    blocks = half // 128
    base = base_ref[0]
    for part in range(2):
        goal = lane_row(target_ref, part * blocks, blocks) - base
        weight = lane_row(weight_ref, part * blocks, blocks)
        log_total = lane_row(log_ref, part * blocks, blocks)
        factor = weight * (1.0 + 2.0 * zloss_weight * log_total)

        def fill(index, carry, part=part, goal=goal, weight=weight, log_total=log_total, factor=factor):
            rows = pl.ds(pl.multiple_of(index * step, 16), step)
            place = lax.broadcasted_iota(jnp.int32, (step, 1), 0) + index * step
            value = logit_ref[rows, part * half : (part + 1) * half]
            found = jnp.logical_and(place == goal, place < limit)
            grad = factor * jnp.exp(value - log_total) - jnp.where(found, weight, 0.0)
            glog_ref[rows, part * half : (part + 1) * half] = grad.astype(bf16)
            return carry

        lax.fori_loop(0, table_ref.shape[0] // step, fill, 0)
    for part, ref in ((1, far_ref), (0, own_ref)):
        for k in range(half // 256):
            spot = k * 256
            value = turn_dot(
                glog_ref[:, part * half + spot : part * half + spot + 256], table_ref[...]
            )
            ref[spot : spot + 256, :] = value.astype(ref.dtype)


def head_back(base, targets, weights, logs, table, logits, limit):
    rows, tokens = logits.shape
    model = table.shape[1]
    return pl.pallas_call(
        functools.partial(head_back_kernel, limit, rows // 8),
        out_shape=(
            jax.ShapeDtypeStruct((tokens // 2, model), f32),
            jax.ShapeDtypeStruct((tokens // 2, model), bf16),
            jax.ShapeDtypeStruct((rows, tokens), bf16),
        ),
        in_specs=[scalar()] + [whole()] * 5,
        out_specs=(whole(), whole(), whole()),
        compiler_params=params(48),
        cost_estimate=SMALL,
    )(base, targets, weights, logs, table, logits)


def high_low(value):
    high = value.astype(bf16)
    return high, (value - high.astype(f32)).astype(bf16)


def inverse_parts(token_refs, scale, out_ref, start_ref, shifted_ref):
    order = out_ref.shape[0]
    step = 256

    def gram_rows(index, top):
        rows = pl.ds(pl.multiple_of(index * step, step), step)
        value = jnp.zeros((step, order), f32)
        for ref in token_refs:
            value += turn_dot(ref[:, rows], ref[...])
        value = value * scale
        out_ref[rows, :] = value
        return jnp.maximum(top, jnp.max(jnp.sum(jnp.abs(value), 1)))

    top = lax.fori_loop(0, order // step, gram_rows, jnp.float32(0.0)) + 1e-06

    def start_rows(index, carry):
        rows = pl.ds(pl.multiple_of(index * step, step), step)
        place = lax.broadcasted_iota(jnp.int32, (step, order), 0) + index * step
        eye = (place == lax.broadcasted_iota(jnp.int32, (step, order), 1)).astype(f32)
        shifted = out_ref[rows, :] / top + damping * eye
        start = 2.0 / kappa * eye - shifted * (1.0 / (kappa * kappa))
        shifted_ref[rows, :] = shifted.astype(bf16)
        start_ref[rows, :] = start.astype(bf16)
        out_ref[rows, :] = 2.0 * start
        return carry

    lax.fori_loop(0, order // step, start_rows, 0)

    def last_rows(index, carry):
        rows = pl.ds(pl.multiple_of(index * step, step), step)
        product = jnp.dot(shifted_ref[rows, :], start_ref[...], preferred_element_type=f32)
        out_ref[rows, :] = out_ref[rows, :] - jnp.dot(
            product.astype(bf16), start_ref[...], preferred_element_type=f32
        )
        return carry

    lax.fori_loop(0, order // step, last_rows, 0)


def pick_columns(inverse_ref, first, lanes):
    order = inverse_ref.shape[0]
    place = lax.broadcasted_iota(jnp.int32, (order, lanes), 0) - first
    chosen = (place == lax.broadcasted_iota(jnp.int32, (order, lanes), 1)).astype(bf16)
    high, rest = high_low(inverse_ref[...])
    return (
        jnp.dot(high, chosen, preferred_element_type=f32).astype(bf16),
        jnp.dot(rest, chosen, preferred_element_type=f32).astype(bf16),
    )


def inverse_kernel(count, scale_ref, *refs):
    out_ref, start_ref, shifted_ref = refs[count:]
    inverse_parts(refs[:count], scale_ref[0], out_ref, start_ref, shifted_ref)


def slim_kernel(count, scale_ref, first_ref, *refs):
    token_refs = refs[:count]
    out_ref, turned_ref, start_ref, shifted_ref = refs[count:]
    inverse_parts(token_refs, scale_ref[0], out_ref, start_ref, shifted_ref)
    high, rest = pick_columns(out_ref, first_ref[0], turned_ref.shape[1])
    base = 0
    for ref in token_refs:
        rows = ref.shape[0]
        turned_ref[base : base + rows, :] = jnp.dot(
            ref[...], high, preferred_element_type=f32
        ) + jnp.dot(ref[...], rest, preferred_element_type=f32)
        base += rows


def pair_kernel(count, scale_ref, first_ref, left_ref, *refs):
    in_refs = refs[:count]
    token_refs = refs[count : 2 * count]
    result_ref, square_ref, out_ref, start_ref, shifted_ref = refs[2 * count :]
    lanes = 128
    inverse_parts(token_refs, scale_ref[0], out_ref, start_ref, shifted_ref)
    high, rest = pick_columns(out_ref, first_ref[0], lanes)
    order = out_ref.shape[0]
    grad = jnp.zeros((lanes, order), f32)
    for in_ref, ref in zip(in_refs, token_refs):
        turned = jnp.dot(ref[...], high, preferred_element_type=f32) + jnp.dot(
            ref[...], rest, preferred_element_type=f32
        )
        turned_high, turned_rest = high_low(turned)
        grad += turn_dot(turned_high, in_ref[...]) + turn_dot(turned_rest, in_ref[...])
    grad_high, grad_rest = high_low(grad)
    left_high, left_rest = high_low(left_ref[...])
    result = (
        far_dot(left_high, grad_high) + far_dot(left_rest, grad_high) + far_dot(left_high, grad_rest)
    )
    result = result[:, : result_ref.shape[1]]
    result_ref[...] = result
    square_ref[0] = jnp.sum(result * result)


def approx_inverse(parts, scale):
    order = parts[0].shape[1]
    count = len(parts)
    rows = sum(part.shape[0] for part in parts)
    return pl.pallas_call(
        functools.partial(inverse_kernel, count),
        out_shape=jax.ShapeDtypeStruct((order, order), f32),
        in_specs=[scalar()] + [whole()] * count,
        out_specs=whole(),
        scratch_shapes=[pltpu.VMEM((order, order), bf16)] * 2,
        compiler_params=params(40),
        cost_estimate=SMALL,
    )(scale, *parts)


def slim_inverse(parts, scale, first):
    order = parts[0].shape[1]
    count = len(parts)
    rows = sum(part.shape[0] for part in parts)
    return pl.pallas_call(
        functools.partial(slim_kernel, count),
        out_shape=(
            jax.ShapeDtypeStruct((order, order), f32),
            jax.ShapeDtypeStruct((rows, 128), f32),
        ),
        in_specs=[scalar()] * 2 + [whole()] * count,
        out_specs=(whole(), whole()),
        scratch_shapes=[pltpu.VMEM((order, order), bf16)] * 2,
        compiler_params=params(40),
        cost_estimate=SMALL,
    )(scale, first, *parts)


def pair_factor(in_parts, out_parts, left, scale, first, columns):
    order = left.shape[0]
    count = len(in_parts)
    rows = sum(part.shape[0] for part in in_parts)
    return pl.pallas_call(
        functools.partial(pair_kernel, count),
        out_shape=(
            jax.ShapeDtypeStruct((order, columns), f32),
            jax.ShapeDtypeStruct((1,), f32),
        ),
        in_specs=[scalar()] * 2 + [whole()] * (1 + 2 * count),
        out_specs=(whole(), scalar()),
        scratch_shapes=[pltpu.VMEM((order, order), f32)] + [pltpu.VMEM((order, order), bf16)] * 2,
        compiler_params=params(48),
        cost_estimate=SMALL,
    )(scale, first, left, *in_parts, *out_parts)


def finish_kernel(
    columns,
    chip_ref,
    coef_ref,
    gram_ref,
    start_ref,
    wide_ref,
    in_ref,
    left_ref,
    down_ref,
    up_ref,
    square_ref,
    total_ref,
    power_ref,
):
    power_ref[...] = start_ref[...]
    total_ref[...] = coef_ref[0] * start_ref[...]
    for step in range(1, 4):
        power_ref[...] = jnp.dot(
            gram_ref[...], power_ref[...].astype(bf16), preferred_element_type=f32
        )
        total_ref[...] += coef_ref[step] * power_ref[...]
    model = in_ref.shape[1]

    @pl.when(chip_ref[0] == 0)
    def _():
        high, rest = high_low(total_ref[:, :128])
        square = jnp.float32(0.0)
        for part in range(2):
            piece = wide_ref[:, part * model : (part + 1) * model]
            result = (turn_dot(high, piece) + turn_dot(rest, piece))[:columns, :]
            down_ref[part] = result
            square += jnp.sum(result * result)
        up_ref[...] = jnp.zeros_like(up_ref)
        square_ref[0] = square

    @pl.when(chip_ref[0] != 0)
    def _():
        high, rest = high_low(total_ref[...])
        turned = turn_dot(in_ref[...], high) + turn_dot(in_ref[...], rest)
        turned_high, turned_rest = high_low(turned)
        left_high, left_rest = high_low(left_ref[...])
        result = (
            jnp.dot(left_high, turned_high, preferred_element_type=f32)
            + jnp.dot(left_rest, turned_high, preferred_element_type=f32)
            + jnp.dot(left_high, turned_rest, preferred_element_type=f32)
        )
        up_ref[...] = result
        down_ref[...] = jnp.zeros_like(down_ref)
        square_ref[0] = jnp.sum(result * result)


def wide_finish(chip, coefs, gram, start, wide, slim_in, left, columns):
    rows, width = start.shape
    model = slim_in.shape[1]
    if not fits(rows):
        return plain_wide_finish(chip, coefs, gram, start, wide, slim_in, left, columns)
    return pl.pallas_call(
        functools.partial(finish_kernel, columns),
        out_shape=(
            jax.ShapeDtypeStruct((2, columns, model), f32),
            jax.ShapeDtypeStruct((left.shape[0], width), f32),
            jax.ShapeDtypeStruct((1,), f32),
        ),
        in_specs=[scalar()] * 2 + [whole()] * 5,
        out_specs=(whole(), whole(), scalar()),
        scratch_shapes=[pltpu.VMEM((rows, width), f32)] * 2,
        compiler_params=params(48),
        cost_estimate=SMALL,
    )(chip, coefs, gram, start, wide, slim_in, left)


def series():
    alpha = 2.0 / kappa - damping / (kappa * kappa)
    beta = 1.0 / (kappa * kappa)
    return (
        2.0 * alpha - damping * alpha * alpha,
        -2.0 * beta - alpha * alpha + 2.0 * alpha * beta * damping,
        2.0 * alpha * beta - damping * beta * beta,
        -beta * beta,
    )


def sum_half(partial, core_bit):
    rows = partial.shape[0]
    halves = partial.reshape(2, rows // 2, partial.shape[1])
    keep = lax.dynamic_index_in_dim(halves, core_bit, 0, False)
    send = lax.dynamic_index_in_dim(halves, 1 - core_bit, 0, False)
    keep = keep + xor_permute(send, "blk", 1)
    return keep + xor_permute(keep, "blk", 2)


def join_half(half, core_bit):
    other = xor_permute(half, "blk", 1)
    both = by_order(core_bit, half, other, 0)
    return both.reshape((2 * half.shape[0],) + half.shape[1:])


def split_dots(left_low, right):
    high = right.astype(bf16)
    rest = (right - high.astype(f32)).astype(bf16)
    return jnp.dot(left_low, high, preferred_element_type=f32) + jnp.dot(
        left_low, rest, preferred_element_type=f32
    )


def body(
    token_ids,
    lengths,
    embedding,
    emb_mean,
    emb_var,
    positions,
    pos_mean,
    pos_var,
    gains_biases,
    gains_mean,
    gains_var,
    w_attn,
    attn_mean,
    attn_var,
    w_fc,
    fc_mean,
    fc_var,
    w_proj,
    proj_mean,
    proj_var,
):
    row_len = token_ids.shape[1]
    piece_rows = embedding.shape[0]
    dp_size = lax.axis_size("dp")
    blk_size = lax.axis_size("blk")
    dp_index = lax.axis_index("dp")
    blk_index = lax.axis_index("blk")
    core_bit = blk_index % 2
    chip_bit = blk_index // 2
    row_bit = dp_index % 2
    tokens = float(row_len * dp_size)
    sub_len = row_len // blk_size
    half_len = row_len // 2
    total_rows = row_len * dp_size
    ff_part = FF // blk_size
    head_cols = D // blk_size
    col_part = D // dp_size
    wide_part = FF // dp_size

    packed = spread_small(jnp.concatenate([token_ids[0], lengths[0]]), "dp")
    every_ids = packed[:, :row_len]
    every_lengths = packed[:, row_len:]
    every_local, every_counted, _ = jax.vmap(lambda row: doc_layout(row, row_len))(every_lengths)
    total_count = jnp.sum(every_counted.astype(f32))
    _, _, attn_mask = doc_layout(lengths[0], row_len)
    every_targets = jnp.concatenate([every_ids[:, 1:], jnp.zeros((dp_size, 1), jnp.int32)], 1)
    row_base = (dp_index * blk_size + blk_index) * piece_rows
    vocab_slots = row_base + jnp.arange(piece_rows, dtype=jnp.int32)
    table_low = embedding.astype(bf16)

    span = dp_size // blk_size
    attn_low = w_attn[0].astype(bf16)
    rows_here = attn_low.shape[0]
    qkv_all = spread(attn_low[:, :3].reshape(rows_here, 3 * col_part), "dp")
    up_low = w_fc[0].astype(bf16)
    down_low = w_proj[0].astype(bf16).reshape(rows_here, wide_part)
    out_low = attn_low[:, 3].reshape(rows_here // 4, wide_part)
    mid_all = lax.all_gather(jnp.concatenate([up_low, out_low], 0), "dp", axis=0)
    down_all = lax.all_gather(down_low, "dp", axis=0)

    def turn(value):
        grouped = value.reshape((blk_size, span) + value.shape[1:])

        def block(index):
            return lax.dynamic_index_in_dim(grouped, index, 0, False)

        found = [block(blk_index)] + [
            xor_permute(block(blk_index ^ k), "blk", k) for k in range(1, blk_size)
        ]
        return jnp.stack(
            [
                jnp.where(
                    chip_bit == 0,
                    jnp.where(core_bit == 0, found[k], found[k ^ 1]),
                    jnp.where(core_bit == 0, found[k ^ 2], found[k ^ 3]),
                )
                for k in range(blk_size)
            ]
        )

    def sub_of(index):
        return (index % 2) * (blk_size // 2) + index // 2

    id_subs = every_ids.reshape(dp_size, blk_size, sub_len)

    def picked(step):
        ids = lax.dynamic_index_in_dim(id_subs, sub_of(blk_index ^ step), 1, False).reshape(-1)
        hit = (ids[:, None] == vocab_slots[None, :]).astype(bf16)
        return jnp.dot(hit, table_low, preferred_element_type=f32).astype(bf16)

    far = jnp.stack([picked(1), picked(3)])
    near = jnp.stack([picked(0), picked(2)])
    near = near + xor_permute(far, "blk", 1)
    embedded_sub = near[0] + xor_permute(near[1], "blk", 2)
    embedded_sub, qkv_all = together(embedded_sub, qkv_all)
    qkv_turn = turn(qkv_all).reshape(blk_size, span, rows_here, 3, col_part)
    w_qkv = jnp.transpose(qkv_turn, (0, 2, 3, 1, 4)).reshape(D, 3, head_cols)
    embedded_sub = lax.all_to_all(
        embedded_sub.reshape(dp_size, sub_len, D), "dp", split_axis=0, concat_axis=0
    )
    embedded_sub = jnp.sum(embedded_sub.astype(f32), 0).astype(bf16)
    embedded = by_order(chip_bit, embedded_sub, xor_permute(embedded_sub, "blk", 2), 0)
    embedded, mid_all = together(embedded, mid_all)
    embedded = embedded.reshape(half_len, D).astype(f32)
    my_local, my_counted, _ = doc_layout(lengths[0], row_len)
    half_start = core_bit * half_len
    local_half = lax.dynamic_slice_in_dim(my_local, half_start, half_len, 0)
    pos_hit = (local_half[:, None] == jnp.arange(row_len, dtype=jnp.int32)[None, :]).astype(f32)
    stream = embedded + jnp.dot(pos_hit, positions, precision=HIGHEST)

    gain_one, shift_one, bias_q, bias_v, bias_o, gain_two, shift_two = (
        gains_biases[k] for k in range(7)
    )
    ff_rows = FF // D
    bias_fc = gains_biases[7 : 7 + ff_rows].reshape(FF)
    bias_proj = gains_biases[7 + ff_rows]
    gain_fin = gains_biases[8 + ff_rows]
    shift_fin = gains_biases[9 + ff_rows]

    def cut(vector, width):
        return lax.dynamic_slice_in_dim(vector, blk_index * width, width, 0)

    w_out = mid_all[:, rows_here:].reshape(dp_size, rows_here, col_part)
    w_out = jnp.transpose(w_out, (1, 0, 2)).reshape(head_cols, D)
    w_up = jnp.transpose(turn(mid_all[:, :rows_here]), (0, 2, 1, 3)).reshape(D, ff_part)
    w_down = down_all.reshape(dp_size, ff_part, col_part)
    w_down = jnp.transpose(w_down, (1, 0, 2)).reshape(ff_part, D)

    def turn_pair(value, axis, bit):
        return jnp.where(bit == 0, value, jnp.flip(value, axis))

    def own_order(value):
        value = value.reshape(dp_size, 2, half_len).transpose(1, 0, 2)
        return turn_pair(value, 0, core_bit).reshape(-1)

    own_ids = own_order(every_ids)
    own_targets = own_order(every_targets)
    own_counted = own_order(every_counted)
    own_local = own_order(every_local)

    token_blocks = total_rows // 128
    block_targets = own_targets.reshape(token_blocks, 128)
    block_counted = own_counted.astype(f32).reshape(token_blocks, 128)

    normed = join_half(layer_norm(stream, gain_one, shift_one).astype(bf16), core_bit)
    bias_q_cut, bias_v_cut = cut(bias_q, head_cols), cut(bias_v, head_cols)
    qkv_bias = jnp.stack([bias_q_cut, jnp.zeros_like(bias_q_cut), bias_v_cut])
    qkv_low = (dot("sd,dke->ske", normed, w_qkv) + qkv_bias).astype(bf16)
    heads_here = head_cols // HDIM
    split = qkv_low.reshape(row_len, 3, heads_here, HDIM)
    score_scale = 1.0 / math.sqrt(HDIM)
    scores = dot("shd,thd->hst", split[:, 0], split[:, 1]) * score_scale
    probs = jax.nn.softmax(jnp.where(attn_mask[None], scores, -1e30), axis=-1)
    probs_low = probs.astype(bf16)
    mixed = dot("hst,thd->shd", probs_low, split[:, 2]).astype(bf16).reshape(row_len, head_cols)
    last = blk_index == blk_size - 1
    mixed_row = jnp.concatenate(
        [xor_permute(mixed, "blk", k) for k in range(blk_size - 1, 0, -1)] + [mixed], 1
    )
    in_row = jnp.where(last, mixed_row, normed)
    mixed_sum = sum_half(jnp.dot(mixed, w_out, preferred_element_type=f32), core_bit)
    mixed_sum, block_targets, block_counted, own_ids, own_local, total_count = together(
        mixed_sum, block_targets, block_counted, own_ids, own_local, total_count
    )
    middle = stream + mixed_sum + bias_o

    normed_two_half = layer_norm(middle, gain_two, shift_two).astype(bf16)
    normed_two = join_half(normed_two_half, core_bit)
    slim_in = lax.all_gather(normed_two, "dp", axis=0).reshape(-1, D)
    hidden = jnp.dot(normed_two, w_up, preferred_element_type=f32) + cut(bias_fc, ff_part)
    active = jax.nn.gelu(hidden, approximate=True).astype(bf16)
    stream_out = (
        middle
        + sum_half(jnp.dot(active, w_down, preferred_element_type=f32), core_bit)
        + bias_proj
    )
    final_half = layer_norm(stream_out, gain_fin, shift_fin).astype(bf16)

    up_far = xor_permute(w_up, "blk", 2)
    down_far = xor_permute(w_down, "blk", 2)
    bias_group = jnp.stack(
        [
            lax.dynamic_slice_in_dim(bias_fc, (blk_index ^ k) * ff_part, ff_part, 0)
            for k in (0, 2, 1, 3)
        ]
    )

    in_side = lax.all_gather(in_row, "dp", axis=0).reshape(-1, D)
    in_scale = 1.0 / tokens
    out_scale = total_count * total_count / tokens
    share = max(256, FF // (2 * dp_size))
    spot = jnp.stack([chip_bit, dp_index % (FF // (2 * share)) * share])

    final_own, final_far = gather_half(final_half)
    final_own, up_far = together(final_own, up_far)
    table_rows = 128 * -(-piece_rows // 128)
    table_pad = jnp.pad(table_low, ((0, table_rows - piece_rows), (0, 0)))
    base_row = row_base.reshape(1).astype(jnp.int32)
    logits, log_here, hit_sum = head_logits(
        base_row, block_targets, block_counted, table_pad, final_own, final_far, piece_rows
    )
    log_every = spread(log_here, ("dp", "blk"))
    log_every, down_far = together(log_every, down_far)
    sources = lax.broadcasted_iota(jnp.int32, (dp_size * blk_size, 1, 1), 0)
    log_every = jnp.where(
        sources % 2 == core_bit, log_every, jnp.roll(log_every, token_blocks // 2, 1)
    )
    log_top = jnp.max(log_every, 0)
    log_total = log_top + jnp.log(jnp.sum(jnp.exp(log_every - log_top[None]), 0))
    loss_rest = jnp.sum(block_counted * (log_total + zloss_weight * log_total * log_total))
    head_own, head_far, glog = head_back(
        base_row,
        block_targets,
        block_counted / total_count,
        log_total,
        table_pad,
        logits,
        piece_rows,
    )
    head_got = xor_permute(head_far, "blk", 1).reshape(dp_size, 2, sub_len, D)
    head_own = head_own.reshape(dp_size, 2, sub_len, D)

    def chip_part(bit):
        return lax.dynamic_index_in_dim(
            head_own, bit, 1, False
        ) + lax.dynamic_index_in_dim(head_got, bit, 1, False).astype(f32)

    head_sent = xor_permute(chip_part(1 - chip_bit).astype(bf16), "blk", 2)
    head_keep = chip_part(chip_bit) + head_sent.astype(f32)
    head_rows = lax.all_to_all(head_keep.astype(bf16), "dp", split_axis=0, concat_axis=0)

    ups = (w_up, up_far, xor_permute(w_up, "blk", 1), xor_permute(up_far, "blk", 1))
    downs = (w_down, down_far, xor_permute(w_down, "blk", 1), xor_permute(down_far, "blk", 1))
    wide = wide_start(spot, bias_group, slim_in, ups)
    head_rows, in_side, wide = together(head_rows, in_side, wide)
    inv_in = approx_inverse((in_side,), jnp.full((1,), in_scale, f32))
    head_sub = jnp.sum(head_rows.astype(f32), 0)
    grad_final = by_order(chip_bit, head_sub, xor_permute(head_sub, "blk", 2), 0)
    grad_final = grad_final.reshape(half_len, D)
    table_grad = jnp.dot(
        glog, jnp.concatenate([final_own, final_far], 0), preferred_element_type=f32
    )[:piece_rows]

    grad_out, d_gain_fin, d_shift_fin = norm_back(stream_out, gain_fin, grad_final)
    grad_proj_half = grad_out.astype(bf16)
    grad_proj = join_half(grad_proj_half, core_bit)
    slim_mine = spread(grad_proj_half, "dp")
    slim_out = by_order(core_bit, slim_mine, xor_permute(slim_mine, "blk", 1), 1).reshape(-1, D)
    col_start = (dp_index * col_part).reshape(1)
    grad_active = dot("sd,fd->sf", grad_proj, w_down)
    _, gelu_pull = jax.vjp(lambda value: jax.nn.gelu(value, approximate=True), hidden)
    grad_fc = gelu_pull(grad_active)[0].astype(bf16)
    back_two = sum_half(dot("sf,df->sd", grad_fc, w_up), core_bit)
    back_two, inv_in = together(back_two, inv_in)
    back_middle, d_gain_two, d_shift_two = norm_back(middle, gain_two, back_two)
    grad_middle = grad_out + back_middle
    grad_attn_half = grad_middle.astype(bf16)
    grad_attn = join_half(grad_attn_half, core_bit)
    grad_mixed = (
        dot("se,de->sd", grad_attn, w_out).astype(bf16).reshape(row_len, heads_here, HDIM)
    )
    grad_value = dot("hst,shd->thd", probs_low, grad_mixed)
    grad_probs = dot("shd,thd->hst", grad_mixed, split[:, 2])
    grad_scores = (
        probs * (grad_probs - jnp.sum(grad_probs * probs, -1, keepdims=True))
    ).astype(bf16)
    grad_query = dot("hst,thd->shd", grad_scores, split[:, 1]) * score_scale
    grad_key = dot("hst,shd->thd", grad_scores, split[:, 0]) * score_scale
    grad_qkv = (
        jnp.stack([grad_query, grad_key, grad_value], 1)
        .reshape(row_len, 3, head_cols)
        .astype(bf16)
    )
    back_one = sum_half(dot("ske,dke->sd", grad_qkv, w_qkv), core_bit)
    slim_scale = jnp.where(chip_bit == 0, out_scale, in_scale).reshape(1)
    slim = jnp.where(chip_bit == 0, slim_out, slim_in)
    inv_slim, start_slim = slim_inverse((slim,), slim_scale, col_start)
    back_one, inv_slim = together(back_one, inv_slim)
    back_stream, d_gain_one, d_shift_one = norm_back(stream, gain_one, back_one)
    grad_stream = grad_middle + back_stream
    grad_embed_half = grad_stream.astype(bf16)

    pair_blocks = jnp.stack([grad_qkv[:, 0], grad_qkv[:, 1], grad_qkv[:, 2], grad_qkv[:, 2]], 0)
    pair_got = lax.all_to_all(pair_blocks, "blk", split_axis=0, concat_axis=0)
    pair_got, table_grad = together(pair_got, table_grad)
    pair_row = jnp.transpose(pair_got, (1, 0, 2)).reshape(row_len, D)
    out_row = jnp.where(last, grad_attn, pair_row)
    out_side = lax.all_gather(out_row, "dp", axis=0).reshape(-1, D)

    wide, out_row, grad_embed_half = together(wide, out_row, grad_embed_half)
    wide, gram, tops_here = wide_back(spot, wide, slim_out, downs, share)
    wide_scale = jnp.where(chip_bit == 0, in_scale, out_scale)
    gram_top = tops_here[0]
    top_part = tops_here[1] * wide_scale
    out_side, gram = together(out_side, gram)
    lead = (chip_bit == 0).astype(f32)

    def column_sum(value):
        return jnp.sum(value.astype(f32), 0, keepdims=True)

    lanes = lax.broadcasted_iota(jnp.int32, (1, D), 1)

    def place(vector):
        return jnp.where(lanes // head_cols == blk_index, jnp.tile(vector, (1, blk_size)), 0.0)

    ff_place = lax.broadcasted_iota(jnp.int32, (ff_rows, 1), 0) // (ff_rows // blk_size)
    small_part = jnp.concatenate(
        [
            lead * d_gain_one,
            lead * d_shift_one,
            place(column_sum(grad_qkv[:, 0])),
            place(column_sum(grad_qkv[:, 2])),
            lead * column_sum(grad_attn_half),
            lead * d_gain_two,
            lead * d_shift_two,
            jnp.where(ff_place == blk_index, column_sum(grad_fc), 0.0),
            lead * column_sum(grad_proj_half),
            lead * d_gain_fin,
            lead * d_shift_fin,
        ],
        0,
    )
    small_count = small_part.shape[0]
    small_part = small_part + xor_permute(small_part, "blk", 1)
    small_part = small_part + xor_permute(small_part, "blk", 2)
    small_part, top_part = together(small_part, top_part)
    small_every = spread(
        jnp.concatenate([small_part, jnp.full((2, D), top_part, f32)], 0), "dp"
    )
    grad_small = jnp.sum(small_every[:, :small_count], 0)
    top_pair = jnp.max(small_every[:, small_count:, :128], (0, 1), keepdims=True)
    wide_top = jnp.maximum(top_pair, xor_permute(top_pair, "blk", 1))[0, 0, 0] + 1e-06

    pre_small, small_square = pair_factor(
        (in_side,), (out_side,), inv_in, out_scale.reshape(1), col_start, col_part
    )
    pre_attn = lax.all_to_all(
        pre_small.reshape(blk_size, head_cols, col_part), "blk", split_axis=0, concat_axis=0
    )
    pre_attn = jnp.transpose(pre_attn, (1, 0, 2))[None]
    start_slim = jnp.pad(start_slim[:, :col_part], ((0, 0), (0, wide_part - col_part)))
    col_block = dp_index * wide_part // ff_part
    place_at = blk_index ^ col_block
    place_at = (place_at % 2) * 2 + place_at // 2
    start_wide = lax.dynamic_slice_in_dim(
        wide, place_at * ff_part + dp_index * wide_part % ff_part, wide_part, 1
    ).astype(f32)
    power = jnp.where(chip_bit == 0, start_slim, start_wide)
    ratio = gram_top * wide_scale / wide_top
    coef = series()
    coefs = jnp.stack(
        [coef[0] * jnp.ones_like(ratio), coef[1] * ratio, coef[2] * ratio**2, coef[3] * ratio**3]
    )
    left_own = lax.dynamic_slice_in_dim(inv_slim, blk_index * head_cols, head_cols, 0)
    left_far = lax.dynamic_slice_in_dim(inv_slim, (blk_index ^ 2) * head_cols, head_cols, 0)
    down_both, up_both, wide_square = wide_finish(
        chip_bit.reshape(1),
        coefs,
        gram,
        power,
        wide,
        slim_in,
        jnp.concatenate([left_own, left_far], 0),
        col_part,
    )
    low_chips = [k for k in range(blk_size) if k < 2]
    pre_proj = jnp.where(
        chip_bit == 0,
        down_both[0],
        lax.ppermute(down_both[1], "blk", [(k, k ^ 2) for k in low_chips]),
    ).T[None]
    pre_fc = jnp.where(
        chip_bit == 0,
        lax.ppermute(up_both[head_cols:], "blk", [(k ^ 2, k) for k in low_chips]),
        up_both[:head_cols],
    )[None]
    squares = small_square[0] + wide_square[0]

    grad_embed = jnp.concatenate(gather_half(grad_embed_half), 0)
    id_hit = (vocab_slots[:, None] == own_ids[None, :]).astype(bf16)
    table_grad = table_grad + jnp.dot(id_hit, grad_embed, preferred_element_type=f32)
    pos_all = (
        jnp.arange(row_len, dtype=jnp.int32)[:, None] == own_local[None, :]
    ).astype(bf16)
    grad_pos = jnp.dot(pos_all, grad_embed, preferred_element_type=f32)

    squares = squares + jnp.sum(table_grad * table_grad)
    lane = lax.broadcasted_iota(jnp.int32, (8, 128), 1)
    every_squares = spread(jnp.where(lane == 0, squares, hit_sum[0]), ("dp", "blk"))[:, 0, :2]
    every_squares = jnp.sum(every_squares, 0)
    loss_sum = loss_rest - every_squares[1]
    all_squares = (
        every_squares[0] + jnp.sum(grad_small * grad_small) + jnp.sum(grad_pos * grad_pos)
    )
    grad_norm = jnp.sqrt(all_squares)
    clip_factor = clip_level / jnp.maximum(grad_norm, clip_level)
    emb_out = adam_update(embedding, emb_mean, emb_var, table_grad, clip_factor, weight_decay)
    pos_out = adam_update(positions, pos_mean, pos_var, grad_pos, clip_factor, weight_decay)
    gains_out = adam_update(gains_biases, gains_mean, gains_var, grad_small, clip_factor, 0.0)
    attn_out = adam_update(w_attn, attn_mean, attn_var, pre_attn, clip_factor, weight_decay)
    fc_out = adam_update(w_fc, fc_mean, fc_var, pre_fc, clip_factor, weight_decay)
    proj_out = adam_update(w_proj, proj_mean, proj_var, pre_proj, clip_factor, weight_decay)
    return (
        (loss_sum, total_count, grad_norm)
        + emb_out
        + pos_out
        + gains_out
        + attn_out
        + fc_out
        + proj_out
    )


def solution(mesh):
    token = P("dp", None)
    table = P(("dp", "blk"), None)
    attn = P(None, "blk", None, "dp")
    flat = P(None, "blk", "dp")
    return jax.shard_map(
        body,
        mesh=mesh,
        in_specs=(token,) * 2
        + (table,) * 3
        + (P(),) * 6
        + (attn,) * 3
        + (flat,) * 6,
        out_specs=(P(),) * 3 + (table,) * 3 + (P(),) * 6 + (attn,) * 3 + (flat,) * 6,
        check_vma=False,
    )
```
